32 devices in a mesh: groups: 1, expert: 32 (over z, y, x, core).
Axes of the slice: x: 2, y: 2, z: 4, core: 2. Of those that a mesh axis runs over, the one named last changes fastest.
Arguments:
- gate_pre: bfloat16 [32, 3072, 640], P(('groups', 'expert')), may hold values from -6 to 6
- up_pre: bfloat16 [32, 3072, 640], P(('groups', 'expert')), may hold values from -6 to 6
- hidden_grad: bfloat16 [32, 3072, 640], P(('groups', 'expert')), may hold values from -6 to 6
- gate_weight: bfloat16 [32, 3584, 640], P('expert'), may hold values from -0.09375 to 0.09375
- up_weight: bfloat16 [32, 3584, 640], P('expert'), may hold values from -0.09375 to 0.09375
- routes: int32 [4096, 8], P(('groups', 'expert')), may hold values from 0 to 15, all different within a row; in each aligned block of 128 rows (0 to 127, 128 to 255, ...) at most 96 rows name the same one
Outputs:
- token_grad: bfloat16 [4096, 3584], P(('groups', 'expert'))
The draws below stay inside these ranges and needn't reach their ends.
Inputs may be any that keep to these rules, and one draw needn't show every extreme that they name: `routes`: each row names 8 different experts. Among the rows of one device no expert is named more than 96 times, and in every draw some expert is named exactly 96 times by the rows of some device.
All inputs are finite; a program needn't handle non-finite values.
Results may differ from the reference program's by a relative error of at most 0.012.
Values may be sent and summed in bfloat16 or wider, within the bound.
No kernel may reach another device: no remote copies, remote signals or barrier semaphores. Data moves between devices by JAX's collectives and lax.ppermute only.
A program may use at most 192 MiB of HBM per device.

```python
import math
import jax
import jax.numpy as jnp
import numpy as np
from jax import lax

D = 3584
TOPK = 8
TOK_DEV = 128
TOKENS = 4096
EXPERTS = 16
FFH = 640
CAP = 96
SLOTS = 3072
SLICES = 32
N_EXPERT = 32


def level_of(key, shape, cuts, low, high):
    factor_of, own = 1.0, jax.random.fold_in(key, 6)
    for position, shards_of in cuts:
        draws = jnp.exp(jax.random.uniform(jax.random.fold_in(own, position), (shards_of,), jnp.float32, low / len(cuts), high / len(cuts)))
        factor_of = factor_of * jnp.repeat(draws, shape[position] // shards_of).reshape([-1 if axis == position else 1 for axis in range(len(shape))])
    return factor_of


def shared_out(own_key, own, number, rows, number_of, top, limit, slope):
    sequence = jax.random.permutation(own_key, number_of)
    heavy_load, usual = shares(number_of, rows * top, limit, slope, True), shares(number_of, rows * top, limit, slope, False)
    places = jnp.arange(number_of)

    def named(tallies, turn):
        used = int((tallies > 0).sum())
        fixed = max(1, used // 4)
        passed = fixed + (places - fixed + turn * (used - fixed)) % max(1, number_of - fixed)
        return jnp.zeros((number_of,), jnp.int32).at[sequence[jnp.where(places < fixed, places, passed)]].set(jnp.asarray(tallies, jnp.int32))

    tallies = jnp.where(number % 4 == 0, named(heavy_load, number // 4), named(usual, number - number // 4 - 1))
    mixed = jax.random.permutation(jax.random.fold_in(own, 3), number_of)
    giver, taker = mixed[0:number_of // 2 * 2:2], mixed[1:number_of // 2 * 2:2]
    slack = jnp.minimum(tallies[giver] - 1, limit - tallies[taker]) // 2
    slack = jnp.where((giver == sequence[0]) | (taker == sequence[0]) | (tallies[taker] == 0), 0, jnp.maximum(slack, 0))
    passed = jax.random.randint(jax.random.fold_in(own, 4), (number_of // 2,), 0, 1 << 20) % (slack + 1)
    tallies = tallies.at[giver].add(-passed).at[taker].add(passed)
    members = jnp.searchsorted(jnp.cumsum(tallies), jnp.arange(rows * top), side="right").astype(jnp.int32)
    listing = members.reshape(top, rows).T
    listing = listing[jax.random.permutation(jax.random.fold_in(own, 1), rows)]
    turn = jax.random.randint(jax.random.fold_in(own, 2), (rows, 1), 0, top)
    return jnp.take_along_axis(listing, (jnp.arange(top)[None, :] + turn) % top, axis=1)


def shares(count, total, reach, lean, full):
    loads = [(1 << 20) // math.isqrt(grade ** lean) + 1 for grade in range(1, count + 1)]
    largest = reach if full else min(reach, max(-(-total // count), total * loads[0] // sum(loads)))
    least = 1 if total - largest >= count - 1 else 0
    holding, surplus = [largest] + [least] * (count - 1), total - largest - least * (count - 1)
    while surplus > 0:
        candidates = [i for i in range(1, count) if holding[i] < largest] or [i for i in range(1, count) if holding[i] < reach]
        pool, budget = sum([loads[i] for i in candidates]), surplus
        for i in candidates:
            more = min(reach - holding[i], max(1, budget * loads[i] // pool), surplus)
            holding[i] = holding[i] + more
            surplus = surplus - more
    return np.array(holding)


def gaussian(key, shape, width, limit, shards=(), kind=jnp.bfloat16):
    factor_of = level_of(key, shape, shards, -0.22, 0.18) if shards else 1.0
    array = jax.random.normal(key, shape, jnp.float32) * width * factor_of
    return jnp.minimum(jnp.maximum(array, -limit), limit).astype(kind)


def setup_inputs(seed: int = 0, part: int = 0) -> dict:
    arg_keys = jax.random.split(jax.random.key(seed), 7)
    part_splits = jax.random.split(jax.random.fold_in(arg_keys[6], part), 7)
    gate_pre = gaussian(part_splits[0], (SLICES, SLOTS, FFH), 1.0, 6.0, ((0, 32),))
    up_pre = gaussian(part_splits[1], (SLICES, SLOTS, FFH), 1.0, 6.0, ((0, 32),))
    hidden_grad = gaussian(part_splits[2], (SLICES, SLOTS, FFH), 1.0, 6.0, ((0, 32),))
    gate_weight = gaussian(arg_keys[3], (SLICES, D, FFH), D ** -0.5, 0.09375, ((0, 32),))
    up_weight = gaussian(arg_keys[4], (SLICES, D, FFH), D ** -0.5, 0.09375, ((0, 32),))
    routes_keys = jax.random.split(jax.random.fold_in(part_splits[5], 1), TOKENS // TOK_DEV)
    routes_turns = jax.random.permutation(jax.random.fold_in(part_splits[5], 3), TOKENS // TOK_DEV)
    routes = jax.vmap(lambda own, number: shared_out(jax.random.fold_in(part_splits[5], 2), own, number, TOK_DEV, EXPERTS, TOPK, CAP, 2))(routes_keys, routes_turns).reshape((TOKENS, TOPK))
    return {"gate_pre": gate_pre, "up_pre": up_pre, "hidden_grad": hidden_grad, "gate_weight": gate_weight, "up_weight": up_weight, "routes": routes}


def slot_table(routes):
    blocks = routes.reshape(N_EXPERT, TOK_DEV * TOPK)
    picked = (blocks[:, :, None] == jnp.arange(EXPERTS, dtype=jnp.int32)[None, None, :]).astype(jnp.int32)
    before = jnp.cumsum(picked, axis=1) - picked
    slot_ids = jnp.sum(before * picked, axis=2)
    return slot_ids.reshape(TOKENS, TOPK).astype(jnp.int32)


def swiglu_grads(gate_pre, up_pre, hidden_grad):
    gate_values = gate_pre.astype(jnp.float32)
    up_values = up_pre.astype(jnp.float32)
    grad_values = hidden_grad.astype(jnp.float32)
    sigmoid_gate = jax.nn.sigmoid(gate_values)
    grad_gate = grad_values * up_values * sigmoid_gate * (1.0 + gate_values * (1.0 - sigmoid_gate))
    grad_up = grad_values * gate_values * sigmoid_gate
    return grad_gate.astype(jnp.bfloat16), grad_up.astype(jnp.bfloat16)


def slice_partial(gate_pre, up_pre, hidden_grad, gate_weight, up_weight):
    grad_gate, grad_up = swiglu_grads(gate_pre, up_pre, hidden_grad)
    dims = (((1,), (1,)), ((), ()))
    partial_value = lax.dot_general(grad_gate, gate_weight, dims, preferred_element_type=jnp.float32)
    partial_value = partial_value + lax.dot_general(grad_up, up_weight, dims, preferred_element_type=jnp.float32)
    return partial_value.astype(jnp.bfloat16)


def reference(gate_pre, up_pre, hidden_grad, gate_weight, up_weight, routes):
    def per_expert(expert_id):
        pieces = []
        for which_half in range(2):
            slice_id = 2 * expert_id + which_half
            piece = slice_partial(gate_pre[slice_id], up_pre[slice_id], hidden_grad[slice_id], gate_weight[slice_id], up_weight[slice_id])
            pieces.append(piece.astype(jnp.float32))
        return (pieces[0] + pieces[1]).astype(jnp.bfloat16)

    expert_rows = lax.map(per_expert, jnp.arange(EXPERTS, dtype=jnp.int32))
    slot_ids = slot_table(routes)
    source = (jnp.arange(TOKENS, dtype=jnp.int32) // TOK_DEV)[:, None]
    flat_rows = (routes * SLOTS + source * CAP + slot_ids).astype(jnp.int32)
    row_table = expert_rows.reshape(EXPERTS * SLOTS, D)
    gathered = jnp.take(row_table, flat_rows.reshape(-1), axis=0).reshape(TOKENS, TOPK, D)
    return jnp.sum(gathered.astype(jnp.float32), axis=1).astype(jnp.bfloat16)
```

```python
import functools

import jax
import jax.numpy as jnp
from jax import lax
from jax.experimental import pallas as pl
from jax.experimental.pallas import tpu as pltpu
from jax.sharding import PartitionSpec as P

X, Y, Z0, Z1 = 8, 4, 2, 1
MASK = {X: 2, Y: 4, Z0: 8, Z1: 16}
WAVES = (
    (((X, Y, Z0, Z1), (Y, X, Z0, Z1)), 640),
    (((Z0, X, Y, Z1), (Z0, Y, X, Z1)), 512),
    (((X, Y, Z0, Z1), (Y, X, Z0, Z1)), 640),
)
UNIT = 128
VMEM = 60 * 1024 * 1024


def mask_of(position):
    return sum(MASK[bit] for bit in (X, Y, Z0, Z1) if position & bit)


def send(value, mask):
    count = lax.axis_size("expert")
    return lax.ppermute(value, "expert", [(i, i ^ mask) for i in range(count)])


def params(**more):
    return pltpu.CompilerParams(vmem_limit_bytes=VMEM, **more)


def slots_kernel(routes_ref, slot_ref):
    experts, tokens = slot_ref.shape
    chosen = routes_ref.shape[1]
    ids = lax.broadcasted_iota(jnp.int32, (tokens, experts), 1)
    picked = jnp.zeros((tokens, experts), jnp.float32)
    for k in range(chosen):
        picked = picked + (routes_ref[:, k : k + 1] == ids).astype(jnp.float32)
    picked = picked.astype(jnp.bfloat16)
    row = lax.broadcasted_iota(jnp.int32, (tokens, tokens), 0)
    column = lax.broadcasted_iota(jnp.int32, (tokens, tokens), 1)
    dims = (((0,), (0,)), ((), ()))
    before = lax.dot_general(
        picked, (row < column).astype(jnp.bfloat16), dims, preferred_element_type=jnp.float32
    )
    here = lax.dot_general(
        picked, (row == column).astype(jnp.bfloat16), dims, preferred_element_type=jnp.float32
    )
    slot_ref[...] = jnp.where(here > 0.5, before, -1.0).astype(jnp.int32)


def swiglu_kernel(group, table_ref, *refs):
    out_ref = refs[-1]
    width = refs[0].shape[2]
    for i in range(group):
        gate = refs[i][0].astype(jnp.float32)
        up = refs[group + i][0].astype(jnp.float32)
        grad = refs[2 * group + i][0].astype(jnp.float32)
        sigmoid_gate = 0.5 * jnp.tanh(0.5 * gate) + 0.5
        common = grad * sigmoid_gate
        linear = common * gate
        out_ref[i, :, :width] = (up * (common + linear * (1.0 - sigmoid_gate))).astype(
            jnp.bfloat16
        )
        out_ref[i, :, width:] = linear.astype(jnp.bfloat16)


def swiglu(table, gate_pre, up_pre, hidden_grad, group=2):
    count = table.shape[0]
    _, capacity, width = gate_pre.shape
    spec = [
        pl.BlockSpec((1, capacity, width), lambda n, table, i=i: (table[n * group + i], 0, 0))
        for i in range(group)
    ]
    return pl.pallas_call(
        functools.partial(swiglu_kernel, group),
        grid_spec=pltpu.PrefetchScalarGridSpec(
            num_scalar_prefetch=1,
            grid=(count // group,),
            in_specs=spec * 3,
            out_specs=pl.BlockSpec((group, capacity, 2 * width), lambda n, table: (n, 0, 0)),
        ),
        out_shape=jax.ShapeDtypeStruct((count, capacity, 2 * width), jnp.bfloat16),
        compiler_params=params(),
        cost_estimate=pl.CostEstimate(
            flops=20 * count * capacity * width,
            bytes_accessed=10 * count * capacity * width,
            transcendentals=2 * count * capacity * width,
        ),
    )(table, *([gate_pre] * group), *([up_pre] * group), *([hidden_grad] * group))


def rows_kernel(sets, quads, places, steps, *refs):
    count = len(quads)
    own, other, weights = refs[:count], refs[count : 2 * count], refs[2 * count : 2 * count + 4]
    outs, rows = refs[2 * count + 4 : -1], refs[-1]
    pairs, capacity, depth = own[0].shape
    block = pairs * capacity
    n = pl.program_id(0)

    for which in range(2):
        if which and sets[0] == sets[1]:
            continue

        @pl.when(n == which * steps)
        def _():
            for i, q in enumerate(sets[which]):
                at = quads.index(q)
                rows[i * block : (i + 1) * block, :depth] = own[at][...].reshape(block, depth)
                rows[i * block : (i + 1) * block, depth:] = other[at][...].reshape(block, depth)

    dims = (((1,), (1,)), ((), ()))
    width = depth // 2
    total = None
    for i in range(4):
        part = lax.dot_general(
            rows[:, i * width : (i + 1) * width],
            weights[i][...],
            dims,
            preferred_element_type=jnp.float32,
        )
        total = part if total is None else total + part
    total = total.astype(jnp.bfloat16)
    for which in range(2):

        @pl.when((n >= steps) == bool(which))
        def _():
            for i, place in enumerate(places[which]):
                outs[which][place] = total[i * capacity : (i + 1) * capacity]


def expert_rows(own, other, weights, orders, sent, start, columns):
    _, capacity, depth = own.shape
    tile = next(t for t in (640, 512, 384, 256, 128) if columns % t == 0 and start % t == 0 and t <= 320)
    steps = columns // tile
    sets = [[q for q in range(8) if bool(2 * q & order[0]) == sent] for order in orders]
    places = [
        [
            sum(4 >> k for k in range(3) if position & order[k + 1])
            for q in chosen
            for position in (2 * q, 2 * q + 1)
        ]
        for order, chosen in zip(orders, sets)
    ]
    quads = sorted(set(sets[0]) | set(sets[1]))
    spec = [pl.BlockSpec((2, capacity, depth), lambda n, q=q: (q, 0, 0)) for q in quads]
    first = start // tile
    weight = pl.BlockSpec((tile, depth // 2), lambda n: (first + n, 0))
    return pl.pallas_call(
        functools.partial(rows_kernel, sets, quads, places, steps),
        grid=(2 * steps,),
        in_specs=spec * 2 + [weight] * 4,
        out_specs=[
            pl.BlockSpec((8, capacity, tile), lambda n: (0, 0, jnp.minimum(n, steps - 1))),
            pl.BlockSpec((8, capacity, tile), lambda n: (0, 0, jnp.maximum(n - steps, 0))),
        ],
        out_shape=[jax.ShapeDtypeStruct((8, capacity, columns), jnp.bfloat16)] * 2,
        scratch_shapes=[pltpu.VMEM((8 * capacity, 2 * depth), jnp.bfloat16)],
        compiler_params=params(),
        cost_estimate=pl.CostEstimate(
            flops=2 * 8 * capacity * 2 * depth * 2 * columns,
            bytes_accessed=2 * (8 * capacity * (2 * depth + columns) + 2 * depth * columns),
            transcendentals=0,
        ),
    )(*([own] * len(quads)), *([other] * len(quads)), *weights)


def spread_kernel(places, with_arrived, ids_ref, slot_ref, *refs):
    per = 3 if with_arrived else 2
    outs = refs[2 * per :]
    _, capacity, columns = refs[0].shape
    tokens = slot_ref.shape[2]
    ids = lax.broadcasted_iota(jnp.int32, (capacity, tokens), 0)
    dims = (((0,), (0,)), ((), ()))
    for which in range(2):
        for i, place in enumerate(places[which]):
            total = None
            for side in range(2):
                slot = slot_ref[place, pl.ds(ids_ref[2 * which + side], 1), :]
                pick = (ids == slot).astype(jnp.bfloat16)
                part = lax.dot_general(
                    pick, refs[per * which + side][i], dims, preferred_element_type=jnp.float32
                )
                total = part if total is None else total + part
            if with_arrived:
                total = total + refs[per * which + 2][i].astype(jnp.float32)
            total = total.astype(jnp.bfloat16)
            if with_arrived:
                outs[2 * which + (i >= 2)][i % 2] = total
            else:
                outs[which][i] = total


def token_rows(ids, slots, orders, rows, arrived):
    _, capacity, columns = rows[0].shape
    _, experts, tokens = slots.shape
    half = 0 if arrived else 1
    places = [
        [
            sum(order[k + 1] for k in range(3) if (i + 4 * half) & (4 >> k))
            for i in range(4)
        ]
        for order in orders
    ]
    steps = 1 if columns % 256 else 2
    tile = columns // steps
    block = pl.BlockSpec((4, capacity, tile), lambda n, ids: (half, 0, n))
    specs, arguments = [], []
    for which in range(2):
        specs += [block, block]
        arguments += rows[2 * which : 2 * which + 2]
        if arrived:
            specs.append(pl.BlockSpec((4, tokens, tile), lambda n, ids: (0, 0, n)))
            arguments.append(arrived[which])
    blocks, outs = (2, 4) if arrived else (4, 2)
    return pl.pallas_call(
        functools.partial(spread_kernel, places, bool(arrived)),
        grid_spec=pltpu.PrefetchScalarGridSpec(
            num_scalar_prefetch=1,
            grid=(steps,),
            in_specs=[pl.BlockSpec(slots.shape, lambda n, ids: (0, 0, 0))] + specs,
            out_specs=[pl.BlockSpec((blocks, tokens, tile), lambda n, ids: (0, 0, n))] * outs,
        ),
        out_shape=[jax.ShapeDtypeStruct((blocks, tokens, columns), jnp.bfloat16)] * outs,
        compiler_params=params(),
        cost_estimate=pl.CostEstimate(
            flops=32 * capacity * tokens * columns,
            bytes_accessed=64 * tokens * columns,
            transcendentals=0,
        ),
    )(ids, slots, *arguments)


def local(gate_pre, up_pre, hidden_grad, gate_weight, up_weight, routes):
    devices = lax.axis_size("expert")
    experts = devices // 2
    tokens = routes.shape[0]
    capacity = gate_pre.shape[1] // devices
    hidden = gate_pre.shape[2]
    me = lax.axis_index("expert").astype(jnp.int32)

    slots = pl.pallas_call(
        slots_kernel, out_shape=jax.ShapeDtypeStruct((experts, tokens), jnp.int32)
    )(routes)[None]
    for bit in (Z1, Z0, Y, X):
        slots = jnp.concatenate([slots, send(slots, MASK[bit])], axis=0)

    inputs = [v.reshape(devices, capacity, hidden) for v in (gate_pre, up_pre, hidden_grad)]
    masks = jnp.array([mask_of(p) for p in range(16)], jnp.int32)
    weights = [gate_weight[0], up_weight[0]]
    other_weights = [send(w, 1) for w in weights]
    other = send(swiglu((me ^ 1) ^ masks, *inputs), 1)
    own = swiglu(me ^ masks, *inputs)
    weights = weights + other_weights

    waves = []
    start = 0
    for orders, columns in WAVES:
        sent = expert_rows(own, other, weights, orders, True, start, columns)
        waves.append((start, [send(v, MASK[order[0]]) for v, order in zip(sent, orders)]))
        start += 2 * columns
    sums = []
    for (orders, columns), (start, arrived) in zip(WAVES, waves):
        kept = expert_rows(own, other, weights, orders, False, start, columns)
        rows = [kept[0], arrived[0], kept[1], arrived[1]]
        ids = jnp.stack([(me ^ m) // 2 for order in orders for m in (0, MASK[order[0]])])
        upper = token_rows(ids, slots, orders, rows, None)
        sums.append((ids, rows, [send(v, MASK[order[1]]) for v, order in zip(upper, orders)]))
    results = []
    for (orders, columns), (ids, rows, arrived) in zip(WAVES, sums):
        lower = token_rows(ids, slots, orders, rows, arrived)
        for which, order in enumerate(orders):
            third = send(lower[2 * which + 1], MASK[order[2]])
            rest = lower[2 * which].astype(jnp.float32) + third.astype(jnp.float32)
            fourth = send(rest[1].astype(jnp.bfloat16), MASK[order[3]])
            results.append((rest[0] + fourth.astype(jnp.float32)).astype(jnp.bfloat16))
    return jnp.concatenate(results, axis=1)


def solution(mesh):
    placed = (
        P(("groups", "expert"), None, None),
        P(("groups", "expert"), None, None),
        P(("groups", "expert"), None, None),
        P("expert", None, None),
        P("expert", None, None),
        P(("groups", "expert"), None),
    )
    return jax.shard_map(
        local, mesh=mesh, in_specs=placed, out_specs=P(("groups", "expert"), None), check_vma=False
    )
```

```python
import functools

import jax
import jax.numpy as jnp
from jax import lax
from jax.experimental import pallas as pl
from jax.experimental.pallas import tpu as pltpu
from jax.sharding import PartitionSpec as P

X, Y, Z0, Z1 = 8, 4, 2, 1
MASK = {X: 2, Y: 4, Z0: 8, Z1: 16}
TABLE = {X: 1, Y: 2, Z0: 4, Z1: 8}
AM = (X, Y, Z0, Z1), (Y, X, Z1, Z0)
AH = (X, Y, Z0, Z1), (Y, X, Z0, Z1)
BH = (Z0, X, Y, Z1), (Z0, Y, X, Z1)
BZ = (Z0, X, Z1, Y), (Z0, Y, Z1, X)
D = (X, Z0, Y, Z1), (Y, Z0, X, Z1)
E = (X, Z0, Z1, Y), (Y, Z0, Z1, X)
WAVES = ((AH, 512), (BZ, 256), (AH, 512), (BH, 256), (D, 256))
SCHEDULE = (
    *("A0", "S0", "A1", "S1", "S2", "B0", "S3", "B3", "B2", "C0", "B1", "C3", "D0", "B4", "C1", "C2"),
    *("E0", "C4", "D1", "F0", "D3", "D4", "D2", "E1", "E3", "E4", "E2", "F3", "F4", "F2", "F1"),
)
TILE = 256


def mask_of(position):
    return sum(MASK[bit] for bit in (X, Y, Z0, Z1) if position & bit)


def send(value, mask):
    count = lax.axis_size("expert")
    return lax.ppermute(value, "expert", [(i, i ^ mask) for i in range(count)])


def params(mebibytes):
    return pltpu.CompilerParams(vmem_limit_bytes=mebibytes * 1024 * 1024)


HBM, INSIDE = pl.BlockSpec(memory_space=pltpu.HBM), pl.BlockSpec(memory_space=pltpu.VMEM)


def inside(*shape):
    return pltpu.VMEM(shape, jnp.bfloat16)


def slots_kernel(routes_ref, slot_ref):
    experts, tokens = slot_ref.shape
    chosen = routes_ref.shape[1]
    ids = lax.broadcasted_iota(jnp.int32, (tokens, experts), 1)
    picked = jnp.zeros((tokens, experts), jnp.float32)
    for k in range(chosen):
        picked = picked + (routes_ref[:, k : k + 1] == ids).astype(jnp.float32)
    picked = picked.astype(jnp.bfloat16)
    row = lax.broadcasted_iota(jnp.int32, (tokens, tokens), 0)
    column = lax.broadcasted_iota(jnp.int32, (tokens, tokens), 1)
    dims = (((0,), (0,)), ((), ()))
    before = lax.dot_general(
        picked, (row < column).astype(jnp.bfloat16), dims, preferred_element_type=jnp.float32
    )
    here = lax.dot_general(
        picked, (row == column).astype(jnp.bfloat16), dims, preferred_element_type=jnp.float32
    )
    slot_ref[...] = jnp.where(here > 0.5, before, -1.0).astype(jnp.int32)


def swiglu_kernel(side, gate_pre, up_pre, hidden_grad, result, values, ready, *refs):
    capacity, width = values.shape[3:]
    out, out_ready = refs if side else (result, None)
    me = lax.axis_index("expert").astype(jnp.int32)
    core, plane, layer = (me & 1) ^ side, (me >> 1) & 3, me >> 3

    def in_copies(group):
        chip = plane ^ (group >> 1) ^ ((group & 1) << 1)
        for k, source in enumerate((gate_pre, up_pre, hidden_grad)):
            yield pltpu.make_async_copy(
                source.at[:, chip, core], values.at[k, group], ready.at[k, group]
            )

    def out_copy(group):
        rows = pl.ds(4 * group * capacity, 4 * capacity)
        return pltpu.make_async_copy(out.at[rows], result.at[rows], out_ready.at[group])

    for group in range(4):
        for copy in in_copies(group):
            copy.start()
    for group in range(4):
        for copy in in_copies(group):
            copy.wait()

        @pl.loop(0, 4)
        def _(i):
            at = layer ^ (i >> 1) ^ ((i & 1) << 1)
            gate, up, grad = (values[k, group, at].astype(jnp.float32) for k in range(3))
            sigmoid_gate = 0.5 * jnp.tanh(0.5 * gate) + 0.5
            common = grad * sigmoid_gate
            linear = common * gate
            full = up * (common + linear * (1.0 - sigmoid_gate))
            rows = pl.ds(pl.multiple_of((4 * group + i) * capacity, capacity), capacity)
            out[rows, :width] = full.astype(jnp.bfloat16)
            out[rows, width:] = linear.astype(jnp.bfloat16)

        if side:
            out_copy(group).start()
    if side:
        for group in range(4):
            out_copy(group).wait()


def swiglu(side, gate_pre, up_pre, hidden_grad):
    layers, chips, _, capacity, width = gate_pre.shape
    rows = layers * chips * capacity
    scratch_shapes = [
        pltpu.VMEM((3, chips, layers, capacity, width), jnp.bfloat16),
        pltpu.SemaphoreType.DMA((3, chips)),
    ]
    if side:
        scratch_shapes += [
            pltpu.VMEM((rows, 2 * width), jnp.bfloat16),
            pltpu.SemaphoreType.DMA((chips,)),
        ]
    return pl.pallas_call(
        functools.partial(swiglu_kernel, side),
        in_specs=[HBM] * 3,
        out_specs=HBM if side else INSIDE,
        out_shape=jax.ShapeDtypeStruct((rows, 2 * width), jnp.bfloat16) if side else inside(rows, 2 * width),
        scratch_shapes=scratch_shapes,
        compiler_params=params(62 if side else 57),
        cost_estimate=pl.CostEstimate(
            flops=10 * rows * 2 * width,
            bytes_accessed=5 * rows * 2 * width,
            transcendentals=rows * width,
        ),
    )(gate_pre, up_pre, hidden_grad)


def rows_kernel(orders, first, load, _, own, other, *refs):
    if load:
        weights, (kept, loaded, weight, *sent, weight_ready, other_ready) = refs[:4], refs[4:]
        other_copy = pltpu.make_async_copy(other, loaded, other_ready)
        other = loaded
    else:
        weight, kept, *sent = refs
    depth = own.shape[1]
    width = depth // 2
    tile = weight.shape[1]
    capacity, columns = kept.shape[2:]
    steps = columns // tile

    def weight_copy(t, i):
        return pltpu.make_async_copy(
            weights[i].at[pl.ds(pl.multiple_of(t * tile, tile), tile), :],
            weight.at[t, :, pl.ds(i * width, width)],
            weight_ready.at[t, i],
        )

    def part(t, side):
        at = slice(side * depth, (side + 1) * depth)
        return lax.dot_general(
            (own, other)[side][...],
            weight[first + t, :, at],
            (((1,), (1,)), ((), ())),
            preferred_element_type=jnp.float32,
        )

    def place(order, position):
        return sum(4 >> k for k in range(3) if position & order[k + 1])

    if load:
        other_copy.start()

        @pl.loop(0, weight.shape[0])
        def _(t):
            for i in range(4):
                weight_copy(t, i).start()

    @pl.loop(0, 2 * steps)
    def _(t):
        second = t // steps
        if load:
            for i in range(4):
                weight_copy(t, i).wait()
        total = part(t, 0)
        if load:
            pl.when(t == 0)(other_copy.wait)
        total = (total + part(t, 1)).astype(jnp.bfloat16)
        at = pl.ds(pl.multiple_of((t - second * steps) * tile, tile), tile)
        for which, order in enumerate(orders):

            @pl.when(second == which)
            def _():
                for position in range(16):
                    rows = total[position * capacity : (position + 1) * capacity]
                    if not position & order[0]:
                        kept[which, place(order, position), :, at] = rows
                    elif len(sent) == 1:
                        sent[0][which, place(order, position), :, at] = rows
                    else:
                        sent[which][0, place(order, position), :, at] = rows

    if load:

        @pl.loop(2 * steps, weight.shape[0])
        def _(t):
            for i in range(4):
                weight_copy(t, i).wait()


def expert_rows(token, own, other, weights, orders, start, columns, load):
    rows, depth = own.shape
    capacity = rows // 16
    count = 1 if orders[0][0] == orders[1][0] else 2
    out_shape = [inside(2, 8, capacity, columns)]
    scratch_shapes = []
    if load:
        tiles = weights[0].shape[0] // TILE
        out_shape += [inside(rows, depth), inside(tiles, TILE, 2 * depth)]
        scratch_shapes = [pltpu.SemaphoreType.DMA((tiles, 4)), pltpu.SemaphoreType.DMA]
    out_shape += [inside(3 - count, 8, capacity, columns)] * count
    out = pl.pallas_call(
        functools.partial(rows_kernel, orders, start // TILE, load),
        in_specs=[pl.BlockSpec(memory_space=pl.ANY), INSIDE] + ([HBM] * 5 if load else [INSIDE] * 2),
        out_specs=[INSIDE] * len(out_shape),
        out_shape=out_shape,
        scratch_shapes=scratch_shapes,
        compiler_params=params(33 if load else 10),
        cost_estimate=pl.CostEstimate(
            flops=4 * rows * 2 * depth * columns,
            bytes_accessed=2 * (rows * 2 * columns + 4 * depth * columns),
            transcendentals=0,
        ),
    )(token, own, other, *weights)
    if load:
        return out[0], out[3:], out[1], [out[2]]
    return out[0], out[1:], other, weights


def spread_kernel(orders, half, counts, slots, kept, *refs):
    firsts, refs = refs[: counts[0]], refs[counts[0] :]
    arrived, outs = refs[: counts[1]], refs[counts[1] :]
    capacity = kept.shape[2]
    tokens = slots.shape[2]
    me = lax.axis_index("expert").astype(jnp.int32)
    ids = lax.broadcasted_iota(jnp.int32, (capacity, tokens), 0)
    dims = (((0,), (0,)), ((), ()))

    for which, order in enumerate(orders):
        for i in range(4):
            block = i + 4 * half
            place = sum(TABLE[order[k + 1]] for k in range(3) if block & (4 >> k))
            total = None
            for mask, rows in ((0, kept.at[which]), (MASK[order[0]], stream(firsts, which))):
                slot = slots[place, pl.ds((me ^ mask) // 2, 1), :]
                part = lax.dot_general(
                    (ids == slot).astype(jnp.bfloat16),
                    rows[block],
                    dims,
                    preferred_element_type=jnp.float32,
                )
                total = part if total is None else total + part
            if half == 0:
                total = total + stream(arrived, which)[i].astype(jnp.float32)
            total = total.astype(jnp.bfloat16)
            if half:
                stream(outs, which)[i] = total
            elif i < 2:
                outs[0][which, i] = total
            else:
                stream(outs[1:], which)[i - 2] = total


def token_rows(slots, orders, kept, firsts, arrived):
    capacity, columns = kept.shape[2:]
    tokens = slots.shape[2]
    half = 0 if arrived else 1
    counts = len(firsts), len(arrived or ())
    bit = 2 if arrived else 1
    count = 1 if orders[0][bit] == orders[1][bit] else 2
    blocks = 2 if arrived else 4
    shapes = [inside(3 - count, blocks, tokens, columns)] * count
    if arrived:
        shapes = [inside(2, 2, tokens, columns)] + shapes
    arguments = [slots, kept, *firsts, *(arrived or ())]
    out = pl.pallas_call(
        functools.partial(spread_kernel, orders, half, counts),
        in_specs=[INSIDE] * len(arguments),
        out_specs=[INSIDE] * len(shapes),
        out_shape=shapes,
        compiler_params=params(8),
        cost_estimate=pl.CostEstimate(
            flops=32 * capacity * tokens * columns,
            bytes_accessed=64 * tokens * columns,
            transcendentals=0,
        ),
    )(*arguments)
    return (out[0], out[1:]) if arrived else out


def join_kernel(*refs):
    *parts, out = refs
    first = 0
    for part in parts:
        out[first : first + part.shape[0]] = part[...]
        first += part.shape[0]


def join(*parts):
    shape = (sum(part.shape[0] for part in parts), *parts[0].shape[1:])
    return pl.pallas_call(
        join_kernel,
        in_specs=[INSIDE] * len(parts),
        out_specs=INSIDE,
        out_shape=pltpu.VMEM(shape, parts[0].dtype),
        compiler_params=params(4),
    )(*parts)


def stream(values, which):
    return values[0].at[which] if len(values) == 1 else values[which].at[0]


def add_kernel(counts, _, kept, *refs):
    third, refs = refs[: counts[0]], refs[counts[0] :]
    fourth, outs = refs[: counts[1]], refs[counts[1] :]
    for which in range(2):
        block = 0 if fourth else 1
        total = kept[which, block].astype(jnp.float32)
        total = total + stream(third, which)[block].astype(jnp.float32)
        if fourth:
            total = total + stream(fourth, which)[...].astype(jnp.float32)
        stream(outs, which)[...] = total.astype(jnp.bfloat16)


def add(token, kept, third, fourth, merged):
    _, _, tokens, columns = kept.shape
    shapes = [inside(2, tokens, columns)] if merged else [inside(1, tokens, columns)] * 2
    arguments = [kept, *third, *fourth]
    return pl.pallas_call(
        functools.partial(add_kernel, (len(third), len(fourth))),
        in_specs=[pl.BlockSpec(memory_space=pl.ANY)] + [INSIDE] * len(arguments),
        out_specs=[INSIDE] * len(shapes),
        out_shape=shapes,
        compiler_params=params(4),
    )(token, *arguments)


def after(value, last):
    return value if last is None else lax.optimization_barrier((value, last))[0]


def send_all(values, orders, k):
    if len(values) == 1:
        return [send(values[0], MASK[orders[0][k]])]
    return [send(v, MASK[order[k]]) for v, order in zip(values, orders)]


def local(gate_pre, up_pre, hidden_grad, gate_weight, up_weight, routes):
    devices = lax.axis_size("expert")
    experts = devices // 2
    tokens = routes.shape[0]
    capacity = gate_pre.shape[1] // devices
    hidden = gate_pre.shape[2]

    inputs = [
        v.reshape(devices // 8, 4, 2, capacity, hidden) for v in (gate_pre, up_pre, hidden_grad)
    ]
    weights = [gate_weight[0], up_weight[0]]
    weights = weights + [send(w, 1) for w in weights]
    starts = [2 * sum(columns for _, columns in WAVES[:w]) for w in range(len(WAVES))]
    state = {}
    last = None
    for step in SCHEDULE:
        kind, number = step[0], int(step[1])
        if kind not in "AS":
            orders, columns = WAVES[number]
        if step == "A0":
            last = swiglu(1, after(inputs[0], last), *inputs[1:])
            state["other"] = send(last, 1)
        elif step == "A1":
            last = swiglu(0, after(inputs[0], last), *inputs[1:])
            state["own"] = last
        elif step == "S0":
            last = pl.pallas_call(
                slots_kernel,
                out_shape=jax.ShapeDtypeStruct((experts, tokens), jnp.int32),
                compiler_params=params(4),
            )(after(routes, last))[None]
            state["token"] = last
            state["slots"] = [last, send(last, MASK[X])]
        elif kind == "S":
            here, *arrived = state["slots"]
            last = join(after(here, last), *arrived)
            masks = [(MASK[Y],), (MASK[Z0], MASK[Z1], MASK[Z0] + MASK[Z1]), ()][number - 1]
            state["slots"] = [last] + [send(last, mask) for mask in masks]
        elif kind == "B":
            load = "loaded" not in state
            kept, last, state["other"], weights = expert_rows(
                after(state["token"], last), state["own"], state["other"], weights, orders,
                starts[number], columns, load,
            )
            state["loaded"] = True
            state["rows", number] = kept, send_all(last, orders, 0)
        elif kind == "C":
            last = token_rows(after(state["slots"][0], last), orders, *state["rows", number], None)
            state["second", number] = send_all(last, orders, 1)
        elif kind == "D":
            last = token_rows(
                after(state["slots"][0], last), orders, *state["rows", number], state["second", number]
            )
            state["third", number] = last[0], send_all(last[1], orders, 2)
        elif kind == "E":
            kept, third = state["third", number]
            last = add(after(state["token"], last), kept, third, [], orders[0][3] == orders[1][3])
            state["fourth", number] = kept, third, send_all(last, orders, 3)
        elif kind == "F":
            last = add(after(state["token"], last), *state["fourth", number], True)
            state["result", number] = [last[0][0], last[0][1]]
    return jnp.concatenate([v for w in range(len(WAVES)) for v in state["result", w]], axis=1)


def solution(mesh):
    placed = (
        P(("groups", "expert"), None, None),
        P(("groups", "expert"), None, None),
        P(("groups", "expert"), None, None),
        P("expert", None, None),
        P("expert", None, None),
        P(("groups", "expert"), None),
    )
    return jax.shard_map(
        local, mesh=mesh, in_specs=placed, out_specs=P(("groups", "expert"), None), check_vma=False
    )
```

```python
import functools

import jax
import jax.numpy as jnp
from jax import lax
from jax.experimental import pallas as pl
from jax.experimental.pallas import tpu as pltpu
from jax.sharding import PartitionSpec as P

X, Y, Z0, Z1 = 8, 4, 2, 1
MASK = {X: 2, Y: 4, Z0: 8, Z1: 16}
TABLE = {X: 1, Y: 2, Z0: 4, Z1: 8}
AM = (X, Y, Z0, Z1), (Y, X, Z1, Z0)
AH = (X, Y, Z0, Z1), (Y, X, Z0, Z1)
BH = (Z0, X, Y, Z1), (Z0, Y, X, Z1)
BZ = (Z0, X, Z1, Y), (Z0, Y, Z1, X)
D = (X, Z0, Y, Z1), (Y, Z0, X, Z1)
E = (X, Z0, Z1, Y), (Y, Z0, Z1, X)
WAVES = ((AH, 512), (BH, 256), (E, 256), (AM, 512), (AH, 256))
SCHEDULE = (
    *("A0", "S0", "A1", "S1", "S2", "B0", "S3", "B1", "B2", "C0", "B3", "C2", "C1", "D0", "D2", "C3"),
    *("E0", "E2", "B4", "D3", "F0", "C4", "E3", "D1", "D4", "E1", "F3", "E4", "F1", "F2", "F4"),
)
TILE = 256
LIMITS = 26, 6


def mask_of(position):
    return sum(MASK[bit] for bit in (X, Y, Z0, Z1) if position & bit)


def send(value, mask):
    count = lax.axis_size("expert")
    return lax.ppermute(value, "expert", [(i, i ^ mask) for i in range(count)])


def params(mebibytes):
    return pltpu.CompilerParams(vmem_limit_bytes=mebibytes * 1024 * 1024)


HBM, INSIDE = pl.BlockSpec(memory_space=pltpu.HBM), pl.BlockSpec(memory_space=pltpu.VMEM)


def inside(*shape):
    return pltpu.VMEM(shape, jnp.bfloat16)


def slots_kernel(routes_ref, slot_ref):
    experts, tokens = slot_ref.shape
    chosen = routes_ref.shape[1]
    ids = lax.broadcasted_iota(jnp.int32, (tokens, experts), 1)
    picked = jnp.zeros((tokens, experts), jnp.float32)
    for k in range(chosen):
        picked = picked + (routes_ref[:, k : k + 1] == ids).astype(jnp.float32)
    picked = picked.astype(jnp.bfloat16)
    row = lax.broadcasted_iota(jnp.int32, (tokens, tokens), 0)
    column = lax.broadcasted_iota(jnp.int32, (tokens, tokens), 1)
    dims = (((0,), (0,)), ((), ()))
    before = lax.dot_general(
        picked, (row < column).astype(jnp.bfloat16), dims, preferred_element_type=jnp.float32
    )
    here = lax.dot_general(
        picked, (row == column).astype(jnp.bfloat16), dims, preferred_element_type=jnp.float32
    )
    slot_ref[...] = jnp.where(here > 0.5, before, -1.0).astype(jnp.int32)


def swiglu_kernel(side, gate_pre, up_pre, hidden_grad, result, values, ready, *refs):
    capacity, width = values.shape[3:]
    out, out_ready = refs
    me = lax.axis_index("expert").astype(jnp.int32)
    core, plane, layer = (me & 1) ^ side, (me >> 1) & 3, me >> 3

    def in_copies(group):
        chip = plane ^ (group >> 1) ^ ((group & 1) << 1)
        for k, source in enumerate((gate_pre, up_pre, hidden_grad)):
            yield pltpu.make_async_copy(
                source.at[:, chip, core], values.at[k, group], ready.at[k, group]
            )

    def out_copy(group):
        rows = pl.ds(4 * group * capacity, 4 * capacity)
        return pltpu.make_async_copy(out.at[rows], result.at[rows], out_ready.at[group])

    for group in range(4):
        for copy in in_copies(group):
            copy.start()
    for group in range(4):
        for copy in in_copies(group):
            copy.wait()

        @pl.loop(0, 4)
        def _(i):
            at = layer ^ (i >> 1) ^ ((i & 1) << 1)
            gate, up, grad = (values[k, group, at].astype(jnp.float32) for k in range(3))
            sigmoid_gate = 0.5 * jnp.tanh(0.5 * gate) + 0.5
            common = grad * sigmoid_gate
            linear = common * gate
            full = up * (common + linear * (1.0 - sigmoid_gate))
            rows = pl.ds(pl.multiple_of((4 * group + i) * capacity, capacity), capacity)
            out[rows, :width] = full.astype(jnp.bfloat16)
            out[rows, width:] = linear.astype(jnp.bfloat16)

        out_copy(group).start()
    for group in range(4):
        out_copy(group).wait()


def swiglu(side, gate_pre, up_pre, hidden_grad):
    layers, chips, _, capacity, width = gate_pre.shape
    rows = layers * chips * capacity
    scratch_shapes = [
        pltpu.VMEM((3, chips, layers, capacity, width), jnp.bfloat16),
        pltpu.SemaphoreType.DMA((3, chips)),
        pltpu.VMEM((rows, 2 * width), jnp.bfloat16),
        pltpu.SemaphoreType.DMA((chips,)),
    ]
    return pl.pallas_call(
        functools.partial(swiglu_kernel, side),
        in_specs=[HBM] * 3,
        out_specs=HBM,
        out_shape=jax.ShapeDtypeStruct((rows, 2 * width), jnp.bfloat16),
        scratch_shapes=scratch_shapes,
        compiler_params=params(62),
        cost_estimate=pl.CostEstimate(
            flops=10 * rows * 2 * width,
            bytes_accessed=5 * rows * 2 * width,
            transcendentals=rows * width,
        ),
    )(gate_pre, up_pre, hidden_grad)


def rows_kernel(orders, first, load, _, *refs):
    if load:
        sources, weights, refs = refs[:2], refs[2:6], refs[6:]
        kept, grads, weight, *sent, weight_ready, grads_ready = refs
    else:
        grads, weight, kept, *sent = refs
    depth = grads.shape[2]
    width = depth // 2
    tile = weight.shape[1]
    capacity, columns = kept.shape[2:]
    steps = columns // tile

    def weight_copy(t, i):
        return pltpu.make_async_copy(
            weights[i].at[pl.ds(pl.multiple_of(t * tile, tile), tile), :],
            weight.at[t, :, pl.ds(i * width, width)],
            weight_ready.at[t, i],
        )

    def part(t, side):
        at = slice(side * depth, (side + 1) * depth)
        return lax.dot_general(
            grads[side],
            weight[first + t, :, at],
            (((1,), (1,)), ((), ())),
            preferred_element_type=jnp.float32,
        )

    def place(order, position):
        return sum(4 >> k for k in range(3) if position & order[k + 1])

    def grads_copy(side, i):
        rows = pl.ds(pl.multiple_of(i * capacity, capacity), capacity)
        return pltpu.make_async_copy(
            sources[side].at[rows], grads.at[side, rows], grads_ready.at[side, i]
        )

    def wait_grads(side):
        @pl.loop(0, 16)
        def _(i):
            grads_copy(side, i).wait()

    if load:
        for side in range(2):
            for i in range(2 * side, 2 * side + 2):
                weight_copy(0, i).start()

            @pl.loop(0, 16)
            def _(i):
                grads_copy(side, i).start()

        @pl.loop(1, weight.shape[0])
        def _(t):
            for i in range(4):
                weight_copy(t, i).start()

    @pl.loop(0, 2 * steps)
    def _(t):
        second = t // steps
        if load:
            for i in range(4):
                weight_copy(t, i).wait()
        if load:
            pl.when(t == 0)(lambda: wait_grads(0))
        total = part(t, 0)
        if load:
            pl.when(t == 0)(lambda: wait_grads(1))
        total = (total + part(t, 1)).astype(jnp.bfloat16)
        at = pl.ds(pl.multiple_of((t - second * steps) * tile, tile), tile)
        for which, order in enumerate(orders):

            @pl.when(second == which)
            def _():
                for position in range(16):
                    rows = total[position * capacity : (position + 1) * capacity]
                    if not position & order[0]:
                        kept[which, place(order, position), :, at] = rows
                    elif len(sent) == 1:
                        sent[0][which, place(order, position), :, at] = rows
                    else:
                        sent[which][0, place(order, position), :, at] = rows

    if load:

        @pl.loop(2 * steps, weight.shape[0])
        def _(t):
            for i in range(4):
                weight_copy(t, i).wait()


def expert_rows(token, grads, weights, orders, start, columns):
    load = len(weights) == 4
    rows, depth = grads[0].shape[-2:]
    capacity = rows // 16
    count = 1 if orders[0][0] == orders[1][0] else 2
    out_shape = [inside(2, 8, capacity, columns)]
    scratch_shapes = []
    if load:
        tiles = weights[0].shape[0] // TILE
        out_shape += [inside(2, rows, depth), inside(tiles, TILE, 2 * depth)]
        scratch_shapes = [pltpu.SemaphoreType.DMA((tiles, 4)), pltpu.SemaphoreType.DMA((2, 16))]
    out_shape += [inside(3 - count, 8, capacity, columns)] * count
    arguments = [*grads, *weights]
    out = pl.pallas_call(
        functools.partial(rows_kernel, orders, start // TILE, load),
        in_specs=[pl.BlockSpec(memory_space=pl.ANY)] + [HBM if load else INSIDE] * len(arguments),
        out_specs=[INSIDE] * len(out_shape),
        out_shape=out_shape,
        scratch_shapes=scratch_shapes,
        compiler_params=params(LIMITS[0] if load else LIMITS[1]),
        cost_estimate=pl.CostEstimate(
            flops=4 * rows * 2 * depth * columns,
            bytes_accessed=2 * (rows * 2 * columns + 4 * depth * columns),
            transcendentals=0,
        ),
    )(token, *arguments)
    if load:
        return out[0], out[3:], [out[1]], [out[2]]
    return out[0], out[1:], grads, weights


def spread_kernel(orders, half, counts, slots, kept, *refs):
    firsts, refs = refs[: counts[0]], refs[counts[0] :]
    arrived, outs = refs[: counts[1]], refs[counts[1] :]
    capacity = kept.shape[2]
    tokens = slots.shape[2]
    me = lax.axis_index("expert").astype(jnp.int32)
    ids = lax.broadcasted_iota(jnp.int32, (capacity, tokens), 0)
    dims = (((0,), (0,)), ((), ()))

    for which, order in enumerate(orders):
        for i in range(4):
            block = i + 4 * half
            place = sum(TABLE[order[k + 1]] for k in range(3) if block & (4 >> k))
            total = None
            for mask, rows in ((0, kept.at[which]), (MASK[order[0]], stream(firsts, which))):
                slot = slots[place, pl.ds((me ^ mask) // 2, 1), :]
                part = lax.dot_general(
                    (ids == slot).astype(jnp.bfloat16),
                    rows[block],
                    dims,
                    preferred_element_type=jnp.float32,
                )
                total = part if total is None else total + part
            if half == 0:
                total = total + stream(arrived, which)[i].astype(jnp.float32)
            total = total.astype(jnp.bfloat16)
            if half:
                stream(outs, which)[i] = total
            elif i < 2:
                outs[0][which, i] = total
            else:
                stream(outs[1:], which)[i - 2] = total


def token_rows(slots, orders, kept, firsts, arrived):
    capacity, columns = kept.shape[2:]
    tokens = slots.shape[2]
    half = 0 if arrived else 1
    counts = len(firsts), len(arrived or ())
    bit = 2 if arrived else 1
    count = 1 if orders[0][bit] == orders[1][bit] else 2
    blocks = 2 if arrived else 4
    shapes = [inside(3 - count, blocks, tokens, columns)] * count
    if arrived:
        shapes = [inside(2, 2, tokens, columns)] + shapes
    arguments = [slots, kept, *firsts, *(arrived or ())]
    out = pl.pallas_call(
        functools.partial(spread_kernel, orders, half, counts),
        in_specs=[INSIDE] * len(arguments),
        out_specs=[INSIDE] * len(shapes),
        out_shape=shapes,
        compiler_params=params(8),
        cost_estimate=pl.CostEstimate(
            flops=32 * capacity * tokens * columns,
            bytes_accessed=64 * tokens * columns,
            transcendentals=0,
        ),
    )(*arguments)
    return (out[0], out[1:]) if arrived else out


def join_kernel(*refs):
    *parts, out = refs
    first = 0
    for part in parts:
        out[first : first + part.shape[0]] = part[...]
        first += part.shape[0]


def join(*parts):
    shape = (sum(part.shape[0] for part in parts), *parts[0].shape[1:])
    return pl.pallas_call(
        join_kernel,
        in_specs=[INSIDE] * len(parts),
        out_specs=INSIDE,
        out_shape=pltpu.VMEM(shape, parts[0].dtype),
        compiler_params=params(4),
    )(*parts)


def stream(values, which):
    return values[0].at[which] if len(values) == 1 else values[which].at[0]


def add_kernel(counts, _, kept, *refs):
    third, refs = refs[: counts[0]], refs[counts[0] :]
    fourth, outs = refs[: counts[1]], refs[counts[1] :]
    for which in range(2):
        block = 0 if fourth else 1
        total = kept[which, block].astype(jnp.float32)
        total = total + stream(third, which)[block].astype(jnp.float32)
        if fourth:
            total = total + stream(fourth, which)[...].astype(jnp.float32)
        stream(outs, which)[...] = total.astype(jnp.bfloat16)


def add(token, kept, third, fourth, merged):
    _, _, tokens, columns = kept.shape
    shapes = [inside(2, tokens, columns)] if merged else [inside(1, tokens, columns)] * 2
    arguments = [kept, *third, *fourth]
    return pl.pallas_call(
        functools.partial(add_kernel, (len(third), len(fourth))),
        in_specs=[pl.BlockSpec(memory_space=pl.ANY)] + [INSIDE] * len(arguments),
        out_specs=[INSIDE] * len(shapes),
        out_shape=shapes,
        compiler_params=params(4),
    )(token, *arguments)


def after(value, last):
    return value if last is None else lax.optimization_barrier((value, last))[0]


def send_all(values, orders, k):
    if len(values) == 1:
        return [send(values[0], MASK[orders[0][k]])]
    return [send(v, MASK[order[k]]) for v, order in zip(values, orders)]


def local(gate_pre, up_pre, hidden_grad, gate_weight, up_weight, routes):
    devices = lax.axis_size("expert")
    experts = devices // 2
    tokens = routes.shape[0]
    capacity = gate_pre.shape[1] // devices
    hidden = gate_pre.shape[2]

    inputs = [
        v.reshape(devices // 8, 4, 2, capacity, hidden) for v in (gate_pre, up_pre, hidden_grad)
    ]
    weights = [gate_weight[0], up_weight[0]]
    weights = weights + [send(w, 1) for w in weights]
    starts = [2 * sum(columns for _, columns in WAVES[:w]) for w in range(len(WAVES))]
    state = {}
    last = None
    for step in SCHEDULE:
        kind, number = step[0], int(step[1])
        if kind not in "AS":
            orders, columns = WAVES[number]
        if step == "A0":
            last = swiglu(1, after(inputs[0], last), *inputs[1:])
            state["other"] = send(last, 1)
        elif step == "A1":
            last = swiglu(0, after(inputs[0], last), *inputs[1:])
            state["own"] = last
        elif step == "S0":
            last = pl.pallas_call(
                slots_kernel,
                out_shape=jax.ShapeDtypeStruct((experts, tokens), jnp.int32),
                compiler_params=params(4),
            )(after(routes, last))[None]
            state["token"] = last
            state["slots"] = [last, send(last, MASK[X])]
        elif kind == "S":
            here, *arrived = state["slots"]
            last = join(after(here, last), *arrived)
            masks = [(MASK[Y],), (MASK[Z0], MASK[Z1], MASK[Z0] + MASK[Z1]), ()][number - 1]
            state["slots"] = [last] + [send(last, mask) for mask in masks]
        elif kind == "B":
            grads = state.get("grads") or [state["own"], state["other"]]
            kept, last, state["grads"], weights = expert_rows(
                after(state["token"], last), grads, weights, orders, starts[number], columns
            )
            state["rows", number] = kept, send_all(last, orders, 0)
        elif kind == "C":
            last = token_rows(after(state["slots"][0], last), orders, *state["rows", number], None)
            state["second", number] = send_all(last, orders, 1)
        elif kind == "D":
            last = token_rows(
                after(state["slots"][0], last), orders, *state["rows", number], state["second", number]
            )
            state["third", number] = last[0], send_all(last[1], orders, 2)
        elif kind == "E":
            kept, third = state["third", number]
            last = add(after(state["token"], last), kept, third, [], orders[0][3] == orders[1][3])
            state["fourth", number] = kept, third, send_all(last, orders, 3)
        elif kind == "F":
            last = add(after(state["token"], last), *state["fourth", number], True)
            state["result", number] = [last[0][0], last[0][1]]
    return jnp.concatenate([v for w in range(len(WAVES)) for v in state["result", w]], axis=1)


def solution(mesh):
    placed = (
        P(("groups", "expert"), None, None),
        P(("groups", "expert"), None, None),
        P(("groups", "expert"), None, None),
        P("expert", None, None),
        P("expert", None, None),
        P(("groups", "expert"), None),
    )
    return jax.shard_map(
        local, mesh=mesh, in_specs=placed, out_specs=P(("groups", "expert"), None), check_vma=False
    )
```

```python
import functools

import jax
import jax.numpy as jnp
from jax import lax
from jax.experimental import pallas as pl
from jax.experimental.pallas import tpu as pltpu
from jax.sharding import PartitionSpec as P

X, Y, Z0, Z1 = 8, 4, 2, 1
MASK = {X: 2, Y: 4, Z0: 8, Z1: 16}
TABLE = {X: 1, Y: 2, Z0: 4, Z1: 8}
AM = (X, Y, Z0, Z1), (Y, X, Z1, Z0)
AH = (X, Y, Z0, Z1), (Y, X, Z0, Z1)
BH = (Z0, X, Y, Z1), (Z0, Y, X, Z1)
BZ = (Z0, X, Z1, Y), (Z0, Y, Z1, X)
D = (X, Z0, Y, Z1), (Y, Z0, X, Z1)
E = (X, Z0, Z1, Y), (Y, Z0, Z1, X)
WAVES = ((AH, 512), (BH, 256), (E, 256), (AM, 512), (AM, 256))
SCHEDULE = (
    *("A0", "S0", "A1", "S1", "S2", "B0", "B1", "S3", "B2", "C0", "B3", "C2", "C1", "D0", "D2", "C3"),
    *("E0", "E2", "B4", "D3", "F0", "C4", "E3", "D1", "D4", "E1", "F3", "E4", "F1", "F2", "F4"),
)
TILE = 256
LIMITS = 26, 6


def mask_of(position):
    return sum(MASK[bit] for bit in (X, Y, Z0, Z1) if position & bit)


def send(value, mask):
    count = lax.axis_size("expert")
    return lax.ppermute(value, "expert", [(i, i ^ mask) for i in range(count)])


def params(mebibytes):
    return pltpu.CompilerParams(vmem_limit_bytes=mebibytes * 1024 * 1024)


HBM, INSIDE = pl.BlockSpec(memory_space=pltpu.HBM), pl.BlockSpec(memory_space=pltpu.VMEM)


def inside(*shape):
    return pltpu.VMEM(shape, jnp.bfloat16)


def slots_kernel(routes_ref, slot_ref):
    experts, tokens = slot_ref.shape
    chosen = routes_ref.shape[1]
    ids = lax.broadcasted_iota(jnp.int32, (tokens, experts), 1)
    picked = jnp.zeros((tokens, experts), jnp.float32)
    for k in range(chosen):
        picked = picked + (routes_ref[:, k : k + 1] == ids).astype(jnp.float32)
    picked = picked.astype(jnp.bfloat16)
    row = lax.broadcasted_iota(jnp.int32, (tokens, tokens), 0)
    column = lax.broadcasted_iota(jnp.int32, (tokens, tokens), 1)
    dims = (((0,), (0,)), ((), ()))
    before = lax.dot_general(
        picked, (row < column).astype(jnp.bfloat16), dims, preferred_element_type=jnp.float32
    )
    here = lax.dot_general(
        picked, (row == column).astype(jnp.bfloat16), dims, preferred_element_type=jnp.float32
    )
    slot_ref[...] = jnp.where(here > 0.5, before, -1.0).astype(jnp.int32)


def swiglu_kernel(side, gate_pre, up_pre, hidden_grad, result, values, ready, *refs):
    capacity, width = values.shape[3:]
    out, out_ready = refs
    me = lax.axis_index("expert").astype(jnp.int32)
    core, plane, layer = (me & 1) ^ side, (me >> 1) & 3, me >> 3

    def in_copies(group):
        chip = plane ^ (group >> 1) ^ ((group & 1) << 1)
        for k, source in enumerate((gate_pre, up_pre, hidden_grad)):
            yield pltpu.make_async_copy(
                source.at[:, chip, core], values.at[k, group], ready.at[k, group]
            )

    def out_copy(group):
        rows = pl.ds(4 * group * capacity, 4 * capacity)
        return pltpu.make_async_copy(out.at[rows], result.at[rows], out_ready.at[group])

    for group in range(4):
        for copy in in_copies(group):
            copy.start()
    for group in range(4):
        for copy in in_copies(group):
            copy.wait()

        @pl.loop(0, 4)
        def _(i):
            at = layer ^ (i >> 1) ^ ((i & 1) << 1)
            gate, up, grad = (values[k, group, at].astype(jnp.float32) for k in range(3))
            sigmoid_gate = 0.5 * jnp.tanh(0.5 * gate) + 0.5
            common = grad * sigmoid_gate
            linear = common * gate
            full = up * (common + linear * (1.0 - sigmoid_gate))
            rows = pl.ds(pl.multiple_of((4 * group + i) * capacity, capacity), capacity)
            out[rows, :width] = full.astype(jnp.bfloat16)
            out[rows, width:] = linear.astype(jnp.bfloat16)

        out_copy(group).start()
    for group in range(4):
        out_copy(group).wait()


def swiglu(side, gate_pre, up_pre, hidden_grad):
    layers, chips, _, capacity, width = gate_pre.shape
    rows = layers * chips * capacity
    scratch_shapes = [
        pltpu.VMEM((3, chips, layers, capacity, width), jnp.bfloat16),
        pltpu.SemaphoreType.DMA((3, chips)),
        pltpu.VMEM((rows, 2 * width), jnp.bfloat16),
        pltpu.SemaphoreType.DMA((chips,)),
    ]
    return pl.pallas_call(
        functools.partial(swiglu_kernel, side),
        in_specs=[HBM] * 3,
        out_specs=HBM,
        out_shape=jax.ShapeDtypeStruct((rows, 2 * width), jnp.bfloat16),
        scratch_shapes=scratch_shapes,
        compiler_params=params(62),
        cost_estimate=pl.CostEstimate(
            flops=10 * rows * 2 * width,
            bytes_accessed=5 * rows * 2 * width,
            transcendentals=rows * width,
        ),
    )(gate_pre, up_pre, hidden_grad)


def rows_kernel(orders, first, load, _, *refs):
    if load:
        sources, weights, refs = refs[:2], refs[2:6], refs[6:]
        kept, grads, weight, *sent, weight_ready, grads_ready = refs
    else:
        grads, weight, kept, *sent = refs
    depth = grads.shape[2]
    width = depth // 2
    tile = weight.shape[1]
    capacity, columns = kept.shape[2:]
    steps = columns // tile

    def weight_copy(t, i):
        return pltpu.make_async_copy(
            weights[i].at[pl.ds(pl.multiple_of(t * tile, tile), tile), :],
            weight.at[t, :, pl.ds(i * width, width)],
            weight_ready.at[t, i],
        )

    def part(t, side):
        at = slice(side * depth, (side + 1) * depth)
        return lax.dot_general(
            grads[side],
            weight[first + t, :, at],
            (((1,), (1,)), ((), ())),
            preferred_element_type=jnp.float32,
        )

    def place(order, position):
        return sum(4 >> k for k in range(3) if position & order[k + 1])

    def grads_copy(side, i):
        rows = pl.ds(pl.multiple_of(i * capacity, capacity), capacity)
        return pltpu.make_async_copy(
            sources[side].at[rows], grads.at[side, rows], grads_ready.at[side, i]
        )

    def wait_grads(side):
        @pl.loop(0, 16)
        def _(i):
            grads_copy(side, i).wait()

    if load:
        for side in range(2):
            for i in range(2 * side, 2 * side + 2):
                weight_copy(0, i).start()

            @pl.loop(0, 16)
            def _(i):
                grads_copy(side, i).start()

        @pl.loop(1, weight.shape[0])
        def _(t):
            for i in range(4):
                weight_copy(t, i).start()

    @pl.loop(0, 2 * steps)
    def _(t):
        second = t // steps
        if load:
            for i in range(4):
                weight_copy(t, i).wait()
        if load:
            pl.when(t == 0)(lambda: wait_grads(0))
        total = part(t, 0)
        if load:
            pl.when(t == 0)(lambda: wait_grads(1))
        total = (total + part(t, 1)).astype(jnp.bfloat16)
        at = pl.ds(pl.multiple_of((t - second * steps) * tile, tile), tile)
        for which, order in enumerate(orders):

            @pl.when(second == which)
            def _():
                for position in range(16):
                    rows = total[position * capacity : (position + 1) * capacity]
                    if not position & order[0]:
                        kept[which, place(order, position), :, at] = rows
                    elif len(sent) == 1:
                        sent[0][which, place(order, position), :, at] = rows
                    else:
                        sent[which][0, place(order, position), :, at] = rows

    if load:

        @pl.loop(2 * steps, weight.shape[0])
        def _(t):
            for i in range(4):
                weight_copy(t, i).wait()


def expert_rows(token, grads, weights, orders, start, columns):
    load = len(weights) == 4
    rows, depth = grads[0].shape[-2:]
    capacity = rows // 16
    count = 1 if orders[0][0] == orders[1][0] else 2
    out_shape = [inside(2, 8, capacity, columns)]
    scratch_shapes = []
    if load:
        tiles = weights[0].shape[0] // TILE
        out_shape += [inside(2, rows, depth), inside(tiles, TILE, 2 * depth)]
        scratch_shapes = [pltpu.SemaphoreType.DMA((tiles, 4)), pltpu.SemaphoreType.DMA((2, 16))]
    out_shape += [inside(3 - count, 8, capacity, columns)] * count
    arguments = [*grads, *weights]
    out = pl.pallas_call(
        functools.partial(rows_kernel, orders, start // TILE, load),
        in_specs=[pl.BlockSpec(memory_space=pl.ANY)] + [HBM if load else INSIDE] * len(arguments),
        out_specs=[INSIDE] * len(out_shape),
        out_shape=out_shape,
        scratch_shapes=scratch_shapes,
        compiler_params=params(LIMITS[0] if load else LIMITS[1]),
        cost_estimate=pl.CostEstimate(
            flops=4 * rows * 2 * depth * columns,
            bytes_accessed=2 * (rows * 2 * columns + 4 * depth * columns),
            transcendentals=0,
        ),
    )(token, *arguments)
    if load:
        return out[0], out[3:], [out[1]], [out[2]]
    return out[0], out[1:], grads, weights


def spread_kernel(orders, half, counts, slots, kept, *refs):
    firsts, refs = refs[: counts[0]], refs[counts[0] :]
    arrived, outs = refs[: counts[1]], refs[counts[1] :]
    capacity = kept.shape[2]
    tokens = slots.shape[2]
    me = lax.axis_index("expert").astype(jnp.int32)
    ids = lax.broadcasted_iota(jnp.int32, (capacity, tokens), 0)
    dims = (((0,), (0,)), ((), ()))

    for which, order in enumerate(orders):
        for i in range(4):
            block = i + 4 * half
            place = sum(TABLE[order[k + 1]] for k in range(3) if block & (4 >> k))
            total = None
            for mask, rows in ((0, kept.at[which]), (MASK[order[0]], stream(firsts, which))):
                slot = slots[place, pl.ds((me ^ mask) // 2, 1), :]
                part = lax.dot_general(
                    (ids == slot).astype(jnp.bfloat16),
                    rows[block],
                    dims,
                    preferred_element_type=jnp.float32,
                )
                total = part if total is None else total + part
            if half == 0:
                total = total + stream(arrived, which)[i].astype(jnp.float32)
            total = total.astype(jnp.bfloat16)
            if half:
                stream(outs, which)[i] = total
            elif i < 2:
                outs[0][which, i] = total
            else:
                stream(outs[1:], which)[i - 2] = total


def token_rows(slots, orders, kept, firsts, arrived):
    capacity, columns = kept.shape[2:]
    tokens = slots.shape[2]
    half = 0 if arrived else 1
    counts = len(firsts), len(arrived or ())
    bit = 2 if arrived else 1
    count = 1 if orders[0][bit] == orders[1][bit] else 2
    blocks = 2 if arrived else 4
    shapes = [inside(3 - count, blocks, tokens, columns)] * count
    if arrived:
        shapes = [inside(2, 2, tokens, columns)] + shapes
    arguments = [slots, kept, *firsts, *(arrived or ())]
    out = pl.pallas_call(
        functools.partial(spread_kernel, orders, half, counts),
        in_specs=[INSIDE] * len(arguments),
        out_specs=[INSIDE] * len(shapes),
        out_shape=shapes,
        compiler_params=params(8),
        cost_estimate=pl.CostEstimate(
            flops=32 * capacity * tokens * columns,
            bytes_accessed=64 * tokens * columns,
            transcendentals=0,
        ),
    )(*arguments)
    return (out[0], out[1:]) if arrived else out


def join_kernel(*refs):
    *parts, out = refs
    first = 0
    for part in parts:
        out[first : first + part.shape[0]] = part[...]
        first += part.shape[0]


def join(*parts):
    shape = (sum(part.shape[0] for part in parts), *parts[0].shape[1:])
    return pl.pallas_call(
        join_kernel,
        in_specs=[INSIDE] * len(parts),
        out_specs=INSIDE,
        out_shape=pltpu.VMEM(shape, parts[0].dtype),
        compiler_params=params(4),
    )(*parts)


def stream(values, which):
    return values[0].at[which] if len(values) == 1 else values[which].at[0]


def add_kernel(counts, _, kept, *refs):
    third, refs = refs[: counts[0]], refs[counts[0] :]
    fourth, outs = refs[: counts[1]], refs[counts[1] :]
    for which in range(2):
        block = 0 if fourth else 1
        total = kept[which, block].astype(jnp.float32)
        total = total + stream(third, which)[block].astype(jnp.float32)
        if fourth:
            total = total + stream(fourth, which)[...].astype(jnp.float32)
        stream(outs, which)[...] = total.astype(jnp.bfloat16)


def add(token, kept, third, fourth, merged):
    _, _, tokens, columns = kept.shape
    shapes = [inside(2, tokens, columns)] if merged else [inside(1, tokens, columns)] * 2
    arguments = [kept, *third, *fourth]
    return pl.pallas_call(
        functools.partial(add_kernel, (len(third), len(fourth))),
        in_specs=[pl.BlockSpec(memory_space=pl.ANY)] + [INSIDE] * len(arguments),
        out_specs=[INSIDE] * len(shapes),
        out_shape=shapes,
        compiler_params=params(4),
    )(token, *arguments)


def after(value, last):
    return value if last is None else lax.optimization_barrier((value, last))[0]


def send_all(values, orders, k):
    if len(values) == 1:
        return [send(values[0], MASK[orders[0][k]])]
    return [send(v, MASK[order[k]]) for v, order in zip(values, orders)]


def local(gate_pre, up_pre, hidden_grad, gate_weight, up_weight, routes):
    devices = lax.axis_size("expert")
    experts = devices // 2
    tokens = routes.shape[0]
    capacity = gate_pre.shape[1] // devices
    hidden = gate_pre.shape[2]

    inputs = [
        v.reshape(devices // 8, 4, 2, capacity, hidden) for v in (gate_pre, up_pre, hidden_grad)
    ]
    weights = [gate_weight[0], up_weight[0]]
    weights = weights + [send(w, 1) for w in weights]
    starts = [2 * sum(columns for _, columns in WAVES[:w]) for w in range(len(WAVES))]
    state = {}
    last = None
    for step in SCHEDULE:
        kind, number = step[0], int(step[1])
        if kind not in "AS":
            orders, columns = WAVES[number]
        if step == "A0":
            last = swiglu(1, after(inputs[0], last), *inputs[1:])
            state["other"] = send(last, 1)
        elif step == "A1":
            last = swiglu(0, after(inputs[0], last), *inputs[1:])
            state["own"] = last
        elif step == "S0":
            last = pl.pallas_call(
                slots_kernel,
                out_shape=jax.ShapeDtypeStruct((experts, tokens), jnp.int32),
                compiler_params=params(4),
            )(after(routes, last))[None]
            state["token"] = last
            state["slots"] = [last, send(last, MASK[X])]
        elif kind == "S":
            here, *arrived = state["slots"]
            last = join(after(here, last), *arrived)
            masks = [(MASK[Y],), (MASK[Z0], MASK[Z1], MASK[Z0] + MASK[Z1]), ()][number - 1]
            state["slots"] = [last] + [send(last, mask) for mask in masks]
        elif kind == "B":
            grads = state.get("grads") or [state["own"], state["other"]]
            kept, last, state["grads"], weights = expert_rows(
                after(state["token"], last), grads, weights, orders, starts[number], columns
            )
            state["rows", number] = kept, send_all(last, orders, 0)
        elif kind == "C":
            last = token_rows(after(state["slots"][0], last), orders, *state["rows", number], None)
            state["second", number] = send_all(last, orders, 1)
        elif kind == "D":
            last = token_rows(
                after(state["slots"][0], last), orders, *state["rows", number], state["second", number]
            )
            state["third", number] = last[0], send_all(last[1], orders, 2)
        elif kind == "E":
            kept, third = state["third", number]
            last = add(after(state["token"], last), kept, third, [], orders[0][3] == orders[1][3])
            state["fourth", number] = kept, third, send_all(last, orders, 3)
        elif kind == "F":
            last = add(after(state["token"], last), *state["fourth", number], True)
            state["result", number] = [last[0][0], last[0][1]]
    return jnp.concatenate([v for w in range(len(WAVES)) for v in state["result", w]], axis=1)


def solution(mesh):
    placed = (
        P(("groups", "expert"), None, None),
        P(("groups", "expert"), None, None),
        P(("groups", "expert"), None, None),
        P("expert", None, None),
        P("expert", None, None),
        P(("groups", "expert"), None),
    )
    return jax.shard_map(
        local, mesh=mesh, in_specs=placed, out_specs=P(("groups", "expert"), None), check_vma=False
    )
```
